512 devices in a mesh: dp: 16 (over z_lo, core), mp: 32 (over y, z_hi, x).
Axes of the slice: x: 4, y: 4, z: 16 (z_hi: 2, z_lo: 8; z = z_hi * 8 + z_lo), core: 2. Of those that a mesh axis runs over, the one named last changes fastest.
Arguments:
- acts: bfloat16 [2048, 2688], P('dp', 'mp'), may hold values from -6 to 6
- cotangents: bfloat16 [4, 2048, 2688], P(None, 'dp', 'mp'), may hold values from -1.1953125 to 1.1953125
- w_gate: bfloat16 [2688, 10752], P('dp', 'mp'), may hold values from -0.125 to 0.125
- w_up: bfloat16 [2688, 10752], P('dp', 'mp'), may hold values from -0.125 to 0.125
- w_down: bfloat16 [10752, 2688], P('mp', 'dp'), may hold values from -0.0625 to 0.0625
- unit_rank: int32 [10752], P('mp'), may hold values from 0 to 10751, as said below
Outputs:
- grad_acts: bfloat16 [2048, 2688], P('dp', 'mp')
- grad_gate: bfloat16 [2688, 10752], P('dp', 'mp')
- grad_up: bfloat16 [2688, 10752], P('dp', 'mp')
- grad_down: bfloat16 [10752, 2688], P('mp', 'dp')
The draws below stay inside these ranges and needn't reach their ends.
Inputs may be any that keep to these rules, and one draw needn't show every extreme that they name: unit_rank is a permutation of 0 to 10751. Every block of 336 consecutive units (the units of one index of mp) holds exactly 42 ranks below 1344, 42 ranks from 1344 to below 2688, and 84 ranks from 2688 to below 5376.
All inputs are finite; a program needn't handle non-finite values.
Results may differ from the reference program's by a relative error of at most 0.025.
Values may be sent and summed in bfloat16 or wider, within the bound.
No kernel may reach another device: no remote copies, remote signals or barrier semaphores. Data moves between devices by JAX's collectives and lax.ppermute only.
A program may use at most 64 MiB of HBM per device.

```python
import jax
import jax.numpy as jnp
from jax import lax

D = 2688
FF = 10752
TOK_DEV = 128
BRANCHES = 4
TOKENS = 2048
UNITS_DEV = 336
N_DP = 16


def draw_unit_rank(key, part):
    key = jax.random.fold_in(key, 11)
    blocks = FF // UNITS_DEV
    key_list = jax.random.split(key, 5)
    positions = jax.vmap(lambda one_key: jax.random.permutation(one_key, UNITS_DEV))(jax.random.split(key_list[0], blocks)).astype(jnp.int32)
    band_starts = [0, UNITS_DEV // 8, UNITS_DEV // 4, UNITS_DEV // 2]
    band_sizes = [UNITS_DEV // 8, UNITS_DEV // 8, UNITS_DEV // 4, UNITS_DEV // 2]
    rank_base = [0, FF // 8, FF // 4, FF // 2]
    band_index = (positions >= UNITS_DEV // 8).astype(jnp.int32) + (positions >= UNITS_DEV // 4).astype(jnp.int32) + (positions >= UNITS_DEV // 2).astype(jnp.int32)
    block_ids = jnp.arange(blocks, dtype=jnp.int32)[:, None]
    result = jnp.zeros((blocks, UNITS_DEV), jnp.int32)
    for branch in range(4):
        total_here = blocks * band_sizes[branch]
        inside_index = jnp.clip(block_ids * band_sizes[branch] + positions - band_starts[branch], 0, total_here - 1)
        shuffled = jax.random.permutation(key_list[branch + 1], total_here).astype(jnp.int32)
        result = jnp.where(band_index == branch, rank_base[branch] + jnp.take(shuffled, inside_index), result)
    return result.reshape(FF).astype(jnp.int32)


def spiked(values, rng, source, target, shards_of, factor):
    owner, partner = [(jnp.arange(values.shape[axis_at]) // (values.shape[axis_at] // shards_of)).reshape([-1 if axis == axis_at else 1 for axis in range(values.ndim)]) for axis_at in (source, target)]
    chosen = jax.random.permutation(rng, shards_of)[partner]
    strong = (owner == chosen) | (owner == (partner + shards_of // 2) % shards_of)
    return jnp.where(strong, factor * values, values)


def shard_levels(rng, shape, shards, least, high):
    def one(axis_at, blocks):
        steps = jax.random.uniform(jax.random.fold_in(jax.random.fold_in(rng, 6), axis_at), (blocks,), jnp.float32, least / len(shards), high / len(shards))
        return jnp.repeat(jnp.exp(steps), shape[axis_at] // blocks).reshape((-1,) + (1,) * (len(shape) - axis_at - 1))

    loudness = one(*shards[0])
    for cut in shards[1:]:
        loudness = loudness * one(*cut)
    return loudness


def normal_values(stream_key, dims, scale, most, pieces=(), kind=jnp.bfloat16):
    values = jax.random.normal(stream_key, dims, jnp.float32) * scale
    if len(pieces) > 0:
        values = shard_levels(stream_key, dims, pieces, -0.22, 0.18) * values
    return jnp.clip(values, min=-most, max=most).astype(kind)


def noise_with(own_key, dims, spread, bound, cuts, heavy, kind=jnp.bfloat16):
    drawn = spread * jax.random.normal(own_key, dims, jnp.float32)
    if cuts:
        drawn = drawn * shard_levels(own_key, dims, cuts, -0.22, 0.18)
    return jnp.clip(spiked(drawn, jax.random.fold_in(own_key, 3), *heavy), -bound, bound).astype(kind)


def setup_inputs(seed: int = 0) -> dict:
    streams_of = jax.random.split(jax.random.key(seed), 7)
    return {
        "acts": normal_values(streams_of[0], (TOKENS, D), 1.0, 6.0, ((0, 16), (1, 32))),
        "cotangents": noise_with(streams_of[1], (BRANCHES, TOKENS, D), 0.2, 1.1953125, ((1, 16), (2, 32)), (1, 2, 32, 2.75)),
        "w_gate": normal_values(streams_of[2], (D, FF), D ** -0.5, 0.125, ((0, 16), (1, 32))),
        "w_up": normal_values(streams_of[3], (D, FF), D ** -0.5, 0.125, ((0, 16), (1, 32))),
        "w_down": normal_values(streams_of[4], (FF, D), FF ** -0.5, 0.0625, ((0, 32), (1, 16))),
        "unit_rank": draw_unit_rank(jax.random.fold_in(streams_of[6], 71), 0),
    }


gelu_scale = 0.7978845608028654


def gelu_parts(values):
    tanh_arg = gelu_scale * (values + 0.044715 * values * values * values)
    tanh_val = jnp.tanh(tanh_arg)
    activated = 0.5 * values * (1.0 + tanh_val)
    slope = 0.5 * (1.0 + tanh_val) + 0.5 * values * (1.0 - tanh_val * tanh_val) * gelu_scale * (1.0 + 3.0 * 0.044715 * values * values)
    return activated, slope


def contract_last(left_side, right_side):
    return lax.dot_general(left_side, right_side, (((1,), (1,)), ((), ())), preferred_element_type=jnp.float32)


def contract_first(left_side, right_side):
    return lax.dot_general(left_side, right_side, (((0,), (0,)), ((), ())), preferred_element_type=jnp.float32)


def suffix_sums(cot_all):
    third = cot_all[3].astype(jnp.float32)
    second = cot_all[2].astype(jnp.float32) + third
    first = cot_all[1].astype(jnp.float32) + second
    zeroth = cot_all[0].astype(jnp.float32) + first
    return jnp.stack([zeroth, first, second, third]).astype(jnp.bfloat16)


def reference(acts, cotangents, w_gate, w_up, w_down, unit_rank):
    gate_proj = jnp.dot(acts, w_gate, preferred_element_type=jnp.float32)
    up_proj = jnp.dot(acts, w_up, preferred_element_type=jnp.float32)
    activated, slope = gelu_parts(gate_proj)
    hidden = (activated * up_proj).astype(jnp.bfloat16)
    band_index = (unit_rank >= FF // 8).astype(jnp.int32) + (unit_rank >= FF // 4).astype(jnp.int32) + (unit_rank >= FF // 2).astype(jnp.int32)
    suffix = suffix_sums(cotangents)
    sort_order = jnp.argsort(band_index, stable=True).astype(jnp.int32)
    inverse = jnp.argsort(sort_order, stable=True).astype(jnp.int32)
    band_sizes = [FF // 8, FF // 8, FF // 4, FF // 2]
    down_sorted = jnp.take(w_down, sort_order, axis=0)
    hidden_sorted = jnp.take(hidden, sort_order, axis=1)
    grad_parts = []
    down_parts = []
    offset_at = 0
    for branch in range(4):
        size_here = band_sizes[branch]
        segment = down_sorted[offset_at:offset_at + size_here]
        grad_parts.append(contract_last(suffix[branch], segment))
        hidden_seg = hidden_sorted[:, offset_at:offset_at + size_here].reshape(N_DP, TOK_DEV, size_here)
        suffix_groups = suffix[branch].reshape(N_DP, TOK_DEV, D)

        def group_step(running, group_data):
            hidden_group, suffix_group = group_data
            partial_sum = contract_first(hidden_group, suffix_group)
            rounded = lax.optimization_barrier(partial_sum.astype(jnp.bfloat16))
            return running + rounded.astype(jnp.float32), None

        total_down, _ = lax.scan(group_step, jnp.zeros((size_here, D), jnp.float32), (hidden_seg, suffix_groups))
        down_parts.append(total_down)
        offset_at = offset_at + size_here
    grad_hidden = jnp.take(jnp.concatenate(grad_parts, axis=1), inverse, axis=1)
    grad_down = jnp.take(jnp.concatenate(down_parts, axis=0), inverse, axis=0).astype(jnp.bfloat16)
    grad_gate_hidden = (grad_hidden * up_proj * slope).astype(jnp.bfloat16)
    grad_up_hidden = (grad_hidden * activated).astype(jnp.bfloat16)
    grad_acts = (contract_last(grad_gate_hidden, w_gate) + contract_last(grad_up_hidden, w_up)).astype(jnp.bfloat16)
    grad_gate = contract_first(acts, grad_gate_hidden).astype(jnp.bfloat16)
    grad_up = contract_first(acts, grad_up_hidden).astype(jnp.bfloat16)
    return grad_acts, grad_gate, grad_up, grad_down
```

```python
import jax
import jax.numpy as jnp
from jax import lax
from jax.sharding import Mesh, PartitionSpec as P

FF = 10752
ZL = 8
GELU_SCALE = 0.7978845608028654


def gelu_parts(values):
    tanh_arg = GELU_SCALE * (values + 0.044715 * values * values * values)
    tanh_val = jnp.tanh(tanh_arg)
    activated = 0.5 * values * (1.0 + tanh_val)
    slope = 0.5 * (1.0 + tanh_val) + 0.5 * values * (1.0 - tanh_val * tanh_val) * GELU_SCALE * (
        1.0 + 3.0 * 0.044715 * values * values
    )
    return activated, slope


def dot(left, right, left_dim, right_dim):
    return lax.dot_general(
        left, right, (((left_dim,), (right_dim,)), ((), ())), preferred_element_type=jnp.float32
    )


def suffix_sums(cot_all):
    third = cot_all[3].astype(jnp.float32)
    second = cot_all[2].astype(jnp.float32) + third
    first = cot_all[1].astype(jnp.float32) + second
    zeroth = cot_all[0].astype(jnp.float32) + first
    return [part.astype(jnp.bfloat16) for part in (zeroth, first, second, third)]


def in_order(mine, other, index, axis):
    first = jnp.where(index == 0, mine, other)
    second = jnp.where(index == 0, other, mine)
    return jnp.stack([first, second], axis)


def swap(values, axis_name):
    return lax.ppermute(values, axis_name, [(0, 1), (1, 0)])


def line_gather(shard, place):
    from_left, from_right = [], []
    right = left = shard
    for step in range(ZL - 1):
        right = lax.ppermute(right, "zl", [(i, i + 1) for i in range(step, ZL - 1)])
        left = lax.ppermute(left, "zl", [(i, i - 1) for i in range(1, ZL - step)])
        from_left.append(right)
        from_right.append(left)
    slots = jnp.stack(from_left[::-1] + [shard] + from_right)
    return lax.dynamic_slice_in_dim(slots, ZL - 1 - place, ZL, 0)


def line_scatter(parts, place):
    right = left = None
    for step in range(ZL - 1):
        to_right = parts[jnp.clip(place + ZL - 1 - step, 0, ZL - 1)]
        to_left = parts[jnp.clip(place - ZL + 1 + step, 0, ZL - 1)]
        if step:
            to_right = to_right + right.astype(jnp.float32)
            to_left = to_left + left.astype(jnp.float32)
        right = lax.ppermute(
            to_right.astype(jnp.bfloat16), "zl", [(i, i + 1) for i in range(step + 1)]
        )
        left = lax.ppermute(
            to_left.astype(jnp.bfloat16), "zl", [(i, i - 1) for i in range(ZL - 1 - step, ZL)]
        )
    return parts[place] + right.astype(jnp.float32) + left.astype(jnp.float32)


def per_device(acts, cotangents, w_gate, w_up, w_down, unit_rank):
    place = lax.axis_index("zl")
    core = lax.axis_index("co")
    half = lax.axis_index("zh")
    tokens, features = acts.shape
    units = unit_rank.shape[0]
    rows = w_gate.shape[0]

    weights = jnp.concatenate([w_gate, w_up, w_down.T], 1)
    mine = line_gather(weights, place)
    weights = in_order(mine, swap(mine, "co"), core, 1).reshape(2 * ZL * rows, 3 * units)

    local = jnp.concatenate([acts.T] + [part.T for part in suffix_sums(cotangents)], 1)
    far = swap(local, "zh")

    def spread(values):
        copies = jnp.broadcast_to(values[None], (16,) + values.shape)
        return lax.all_to_all(copies, ("y", "x"), 0, 0).reshape((4, 4) + values.shape)

    near, far = spread(local), spread(far)
    inputs = in_order(near, far, half, 1).reshape(32 * features, 5 * tokens)

    products = dot(inputs, weights, 0, 0)
    gate_proj = products[:tokens, :units]
    up_proj = products[:tokens, units : 2 * units]
    activated, slope = gelu_parts(gate_proj)
    hidden = (activated * up_proj).astype(jnp.bfloat16)
    band = (
        (unit_rank >= FF // 8).astype(jnp.int32)
        + (unit_rank >= FF // 4).astype(jnp.int32)
        + (unit_rank >= FF // 2).astype(jnp.int32)
    )[None, :]
    grad_hidden = jnp.zeros((tokens, units), jnp.float32)
    masked = []
    for branch in range(4):
        rows_of = slice((branch + 1) * tokens, (branch + 2) * tokens)
        grad_hidden = jnp.where(band == branch, products[rows_of, 2 * units :], grad_hidden)
        masked.append(jnp.where(band == branch, hidden, jnp.zeros_like(hidden)))
    masked = jnp.concatenate(masked, 0)
    grad_gate_hidden = (grad_hidden * up_proj * slope).astype(jnp.bfloat16)
    grad_up_hidden = (grad_hidden * activated).astype(jnp.bfloat16)
    both = jnp.concatenate([grad_gate_hidden, grad_up_hidden], 1)

    partial_acts = dot(weights[:, : 2 * units], both, 1, 1).astype(jnp.bfloat16)
    partial_acts = partial_acts.reshape(4, 2, 4, features, tokens).transpose(0, 2, 1, 3, 4)
    partial_acts = partial_acts.reshape(16, 2, features, tokens)
    shares = lax.all_to_all(partial_acts, ("y", "x"), 0, 0)
    shares = jnp.sum(shares.astype(jnp.float32), 0)
    away = swap(shares[1 - half].astype(jnp.bfloat16), "zh")
    grad_acts = (shares[half] + away.astype(jnp.float32)).astype(jnp.bfloat16).T

    wide = jnp.concatenate(
        [
            jnp.pad(both, ((0, 0), (0, units))),
            jnp.pad(masked, ((0, 0), (2 * units, 0))),
        ],
        0,
    )
    partial = dot(inputs, wide, 1, 0).astype(jnp.bfloat16).reshape(ZL, 2, rows, 3 * units)
    kept = jnp.where(core == 0, partial[:, 0], partial[:, 1])
    given = jnp.where(core == 0, partial[:, 1], partial[:, 0])
    parts = kept.astype(jnp.float32) + swap(given, "co").astype(jnp.float32)
    grads = line_scatter(parts, place).astype(jnp.bfloat16)
    return (
        grad_acts,
        grads[:, :units],
        grads[:, units : 2 * units],
        grads[:, 2 * units :].T,
    )


def solution(mesh):
    fine = Mesh(mesh.devices.reshape(ZL, 2, 4, 2, 4), ("zl", "co", "y", "zh", "x"))
    dp, mp = ("zl", "co"), ("y", "zh", "x")
    return jax.shard_map(
        per_device,
        mesh=fine,
        in_specs=(P(dp, mp), P(None, dp, mp), P(dp, mp), P(dp, mp), P(mp, dp), P(mp)),
        out_specs=(P(dp, mp), P(dp, mp), P(dp, mp), P(mp, dp)),
        check_vma=False,
    )
```

```python
import jax
import jax.numpy as jnp
from jax import lax
from jax.sharding import Mesh, PartitionSpec as P

FF = 10752
ZL = 8
GELU_SCALE = 0.7978845608028654


def gelu_parts(values):
    tanh_arg = GELU_SCALE * (values + 0.044715 * values * values * values)
    tanh_val = jnp.tanh(tanh_arg)
    activated = 0.5 * values * (1.0 + tanh_val)
    slope = 0.5 * (1.0 + tanh_val) + 0.5 * values * (1.0 - tanh_val * tanh_val) * GELU_SCALE * (
        1.0 + 3.0 * 0.044715 * values * values
    )
    return activated, slope


def dot(left, right, left_dim, right_dim):
    return lax.dot_general(
        left, right, (((left_dim,), (right_dim,)), ((), ())), preferred_element_type=jnp.float32
    )


def suffix_sums(cot_all):
    third = cot_all[3].astype(jnp.float32)
    second = cot_all[2].astype(jnp.float32) + third
    first = cot_all[1].astype(jnp.float32) + second
    zeroth = cot_all[0].astype(jnp.float32) + first
    return [part.astype(jnp.bfloat16) for part in (zeroth, first, second, third)]


def in_order(mine, other, index, axis):
    first = jnp.where(index == 0, mine, other)
    second = jnp.where(index == 0, other, mine)
    return jnp.stack([first, second], axis)


def swap(values, axis_name):
    return lax.ppermute(values, axis_name, [(0, 1), (1, 0)])


def line_gather(shard, place, ties):
    from_left, from_right = [], []
    right = left = shard
    for step in range(ZL - 1):
        right, left, _ = lax.optimization_barrier((right, left, ties.get(step, ())))
        right = lax.ppermute(right, "zl", [(i, i + 1) for i in range(step, ZL - 1)])
        left = lax.ppermute(left, "zl", [(i, i - 1) for i in range(1, ZL - step)])
        from_left.append(right)
        from_right.append(left)
    slots = jnp.stack(from_left[::-1] + [shard] + from_right)
    return lax.dynamic_slice_in_dim(slots, ZL - 1 - place, ZL, 0)


def line_scatter(parts, place, ties):
    right = left = None
    for step in range(ZL - 1):
        to_right = parts[jnp.clip(place + ZL - 1 - step, 0, ZL - 1)]
        to_left = parts[jnp.clip(place - ZL + 1 + step, 0, ZL - 1)]
        if step:
            to_right = to_right.astype(jnp.float32) + right.astype(jnp.float32)
            to_left = to_left.astype(jnp.float32) + left.astype(jnp.float32)
        to_right, to_left = to_right.astype(jnp.bfloat16), to_left.astype(jnp.bfloat16)
        to_right, to_left, _ = lax.optimization_barrier((to_right, to_left, ties.get(step, ())))
        right = lax.ppermute(to_right, "zl", [(i, i + 1) for i in range(step + 1)])
        left = lax.ppermute(to_left, "zl", [(i, i - 1) for i in range(ZL - 1 - step, ZL)])
    return (
        parts[place].astype(jnp.float32) + right.astype(jnp.float32) + left.astype(jnp.float32)
    )


def per_device(acts, cotangents, w_gate, w_up, w_down, unit_rank):
    place = lax.axis_index("zl")
    core = lax.axis_index("co")
    half = lax.axis_index("zh")
    tokens, features = acts.shape
    units = unit_rank.shape[0]
    rows = w_gate.shape[0]

    local = jnp.concatenate([acts.T] + [part.T for part in suffix_sums(cotangents)], 1)
    far_local = swap(local, "zh")

    def spread(values):
        copies = jnp.broadcast_to(values[None], (16,) + values.shape)
        got = lax.all_to_all(copies, ("y", "x"), 0, 0)
        return got.reshape((4, 2, 2) + values.shape)

    def both_tokens(values):
        kept = lax.dynamic_index_in_dim(values, core, 1, False)
        given = lax.dynamic_index_in_dim(values, 1 - core, 1, False)
        return kept, swap(given, "co")

    near = spread(local)
    near_parts = both_tokens(near)
    far = spread(far_local)
    far_parts = both_tokens(far)
    ties = {1: (far_local,), 3: (near,), 4: near_parts, 5: (far,), 6: far_parts}

    weights = line_gather(jnp.concatenate([w_gate, w_up, w_down.T], 1), place, ties)
    weights = weights.reshape(ZL * rows, 3 * units)
    inputs = in_order(
        jnp.concatenate(near_parts, -1), jnp.concatenate(far_parts, -1), half, 1
    ).reshape(ZL * rows, 10 * tokens)

    band = (
        (unit_rank >= FF // 8).astype(jnp.int32)
        + (unit_rank >= FF // 4).astype(jnp.int32)
        + (unit_rank >= FF // 2).astype(jnp.int32)
    )[None, :]
    products = dot(inputs, weights, 0, 0).reshape(2, 5, tokens, 3 * units)

    def of_bands(group):
        total = jnp.zeros((tokens, units), jnp.float32)
        for branch in range(4):
            total = jnp.where(band == branch, products[group, branch + 1, :, 2 * units :], total)
        return jnp.concatenate([products[group, 0, :, : 2 * units], total], 1)

    sums = of_bands(0) + swap(of_bands(1), "co")
    gate_proj, up_proj, grad_hidden = jnp.split(sums, 3, 1)
    activated, slope = gelu_parts(gate_proj)
    hidden = (activated * up_proj).astype(jnp.bfloat16)
    grad_gate_hidden = (grad_hidden * up_proj * slope).astype(jnp.bfloat16)
    grad_up_hidden = (grad_hidden * activated).astype(jnp.bfloat16)
    own = jnp.concatenate([grad_gate_hidden, grad_up_hidden, hidden], 1)
    other = swap(own, "co")

    def widened(values):
        up_to = jnp.pad(values[:, : 2 * units], ((0, 0), (0, units)))
        masked = [
            jnp.where(band == branch, values[:, 2 * units :], jnp.zeros((), values.dtype))
            for branch in range(4)
        ]
        return [up_to, jnp.pad(jnp.concatenate(masked, 0), ((0, 0), (2 * units, 0)))]

    wide = jnp.concatenate(widened(own) + widened(other), 0)
    parts = dot(inputs, wide, 1, 0).astype(jnp.bfloat16).reshape(ZL, rows, 3 * units)

    gate_up = jnp.concatenate([own[:, : 2 * units], other[:, : 2 * units]], 0)
    partial_acts = dot(weights[:, : 2 * units], gate_up, 1, 1).astype(jnp.bfloat16)
    kept, given = partial_acts[:, :tokens], partial_acts[:, tokens:]
    partial_acts = in_order(kept, swap(given, "co"), core, 0)
    partial_acts = partial_acts.reshape(2, 4, 2, 2, features, tokens)
    partial_acts = partial_acts.transpose(1, 0, 3, 2, 4, 5).reshape(16, 2, features, tokens)
    shares = lax.all_to_all(partial_acts, ("y", "x"), 0, 0)
    shares = jnp.sum(shares.astype(jnp.float32), 0)
    away = swap(shares[1 - half].astype(jnp.bfloat16), "zh")
    grad_acts = (shares[half] + away.astype(jnp.float32)).astype(jnp.bfloat16).T

    grads = line_scatter(parts, place, {3: (shares,), 5: (away,)}).astype(jnp.bfloat16)
    return (
        grad_acts,
        grads[:, :units],
        grads[:, units : 2 * units],
        grads[:, 2 * units :].T,
    )


def solution(mesh):
    fine = Mesh(mesh.devices.reshape(ZL, 2, 4, 2, 4), ("zl", "co", "y", "zh", "x"))
    dp, mp = ("zl", "co"), ("y", "zh", "x")
    return jax.shard_map(
        per_device,
        mesh=fine,
        in_specs=(P(dp, mp), P(None, dp, mp), P(dp, mp), P(dp, mp), P(mp, dp), P(mp)),
        out_specs=(P(dp, mp), P(dp, mp), P(dp, mp), P(mp, dp)),
        check_vma=False,
    )
```

```python
import jax
import jax.numpy as jnp
from jax import lax
from jax.sharding import Mesh, PartitionSpec as P

FF = 10752
ZL = 8
GELU_SCALE = 0.7978845608028654


def gelu_parts(values):
    tanh_arg = GELU_SCALE * (values + 0.044715 * values * values * values)
    tanh_val = jnp.tanh(tanh_arg)
    activated = 0.5 * values * (1.0 + tanh_val)
    slope = 0.5 * (1.0 + tanh_val) + 0.5 * values * (1.0 - tanh_val * tanh_val) * GELU_SCALE * (
        1.0 + 3.0 * 0.044715 * values * values
    )
    return activated, slope


def dot(left, right, left_dim, right_dim):
    return lax.dot_general(
        left, right, (((left_dim,), (right_dim,)), ((), ())), preferred_element_type=jnp.float32
    )


def suffix_sums(cot_all):
    third = cot_all[3].astype(jnp.float32)
    second = cot_all[2].astype(jnp.float32) + third
    first = cot_all[1].astype(jnp.float32) + second
    zeroth = cot_all[0].astype(jnp.float32) + first
    return [part.astype(jnp.bfloat16) for part in (zeroth, first, second, third)]


def in_order(mine, other, index, axis):
    first = jnp.where(index == 0, mine, other)
    second = jnp.where(index == 0, other, mine)
    return jnp.stack([first, second], axis)


def swap(values, axis_name):
    return lax.ppermute(values, axis_name, [(0, 1), (1, 0)])


def line_gather(shard, place, ties):
    from_left, from_right = [], []
    right = left = shard
    carried = {}
    for step in range(ZL - 1):
        if step in ties:
            names, make = ties[step]
            arrays = make(carried)
            right, left, arrays = lax.optimization_barrier((right, left, arrays))
            carried.update(zip(names, arrays))
        else:
            right, left = lax.optimization_barrier((right, left))
        right = lax.ppermute(right, "zl", [(i, i + 1) for i in range(step, ZL - 1)])
        left = lax.ppermute(left, "zl", [(i, i - 1) for i in range(1, ZL - step)])
        from_left.append(right)
        from_right.append(left)
    slots = jnp.stack(from_left[::-1] + [shard] + from_right)
    return lax.dynamic_slice_in_dim(slots, ZL - 1 - place, ZL, 0), carried


def line_scatter(parts, place, ties):
    rows = parts.shape[1]
    cut = rows // 16 * 8
    cuts = ((0, cut), (cut, rows))
    right, left = [None, None], [None, None]
    before = ()
    for step in range(ZL - 1):
        for which, (low, high) in enumerate(cuts):
            to_right = parts[jnp.clip(place + ZL - 1 - step, 0, ZL - 1), low:high]
            to_left = parts[jnp.clip(place - ZL + 1 + step, 0, ZL - 1), low:high]
            if step:
                to_right = to_right.astype(jnp.float32) + right[which].astype(jnp.float32)
                to_left = to_left.astype(jnp.float32) + left[which].astype(jnp.float32)
            to_right, to_left = to_right.astype(jnp.bfloat16), to_left.astype(jnp.bfloat16)
            tie = (before, ties.get(step, ()) if which == 0 else ())
            to_right, to_left, _ = lax.optimization_barrier((to_right, to_left, tie))
            before = (right[1 - which], left[1 - which]) if step else ()
            right[which] = lax.ppermute(to_right, "zl", [(i, i + 1) for i in range(step + 1)])
            left[which] = lax.ppermute(
                to_left, "zl", [(i, i - 1) for i in range(ZL - 1 - step, ZL)]
            )
    own = parts[place].astype(jnp.float32)
    return own + sum(jnp.concatenate(side, 0).astype(jnp.float32) for side in (right, left))


def per_device(acts, cotangents, w_gate, w_up, w_down, unit_rank):
    place = lax.axis_index("zl")
    core = lax.axis_index("co")
    half = lax.axis_index("zh")
    tokens, features = acts.shape
    units = unit_rank.shape[0]
    rows = w_gate.shape[0]

    local = jnp.concatenate([acts.T] + [part.T for part in suffix_sums(cotangents)], 1)
    far_local = swap(local, "zh")

    def spread(values):
        copies = jnp.broadcast_to(values[None], (16,) + values.shape)
        got = lax.all_to_all(copies, ("y", "x"), 0, 0)
        return got.reshape((4, 2, 2) + values.shape)

    def both_tokens(values):
        kept = lax.dynamic_index_in_dim(values, core, 1, False)
        given = lax.dynamic_index_in_dim(values, 1 - core, 1, False)
        return kept, swap(given, "co")

    down = lax.all_gather(w_down.T, "zl").reshape(ZL * rows, units)
    near = spread(local)
    ties = {
        2: (("near", "far_local"), lambda done: (near, far_local)),
        4: (("kept", "given"), lambda done: both_tokens(done["near"])),
        5: (("far",), lambda done: (spread(done["far_local"]),)),
        6: (("far_kept", "far_given"), lambda done: both_tokens(done["far"])),
    }
    gate_up_weights, done = line_gather(jnp.concatenate([w_gate, w_up], 1), place, ties)
    gate_up_weights = gate_up_weights.reshape(ZL * rows, 2 * units)
    inputs = in_order(
        jnp.concatenate([done["kept"], done["given"]], -1),
        jnp.concatenate([done["far_kept"], done["far_given"]], -1),
        half,
        1,
    ).reshape(ZL * rows, 10 * tokens)

    band = (
        (unit_rank >= FF // 8).astype(jnp.int32)
        + (unit_rank >= FF // 4).astype(jnp.int32)
        + (unit_rank >= FF // 2).astype(jnp.int32)
    )[None, :]

    def products(group):
        first = group * 5 * tokens
        gate_up = dot(inputs[:, first : first + tokens], gate_up_weights, 0, 0)
        total = jnp.zeros((tokens, units), jnp.float32)
        by_branch = dot(inputs[:, first + tokens : first + 5 * tokens], down, 0, 0)
        for branch in range(4):
            here = by_branch[branch * tokens : (branch + 1) * tokens]
            total = jnp.where(band == branch, here, total)
        return jnp.concatenate([gate_up, total], 1)

    sums = products(0) + swap(products(1), "co")
    gate_proj, up_proj, grad_hidden = jnp.split(sums, 3, 1)
    activated, slope = gelu_parts(gate_proj)
    hidden = (activated * up_proj).astype(jnp.bfloat16)
    grad_gate_hidden = (grad_hidden * up_proj * slope).astype(jnp.bfloat16)
    grad_up_hidden = (grad_hidden * activated).astype(jnp.bfloat16)
    own = jnp.concatenate([grad_gate_hidden, grad_up_hidden, hidden], 1)
    other = swap(own, "co")

    def widened(values):
        up_to = jnp.pad(values[:, : 2 * units], ((0, 0), (0, units)))
        masked = [
            jnp.where(band == branch, values[:, 2 * units :], jnp.zeros((), values.dtype))
            for branch in range(4)
        ]
        return [up_to, jnp.pad(jnp.concatenate(masked, 0), ((0, 0), (2 * units, 0)))]

    wide = jnp.concatenate(widened(own) + widened(other), 0)
    parts = dot(inputs, wide, 1, 0).astype(jnp.bfloat16).reshape(ZL, rows, 3 * units)

    gate_up = jnp.concatenate([own[:, : 2 * units], other[:, : 2 * units]], 0)
    partial_acts = dot(gate_up_weights, gate_up, 1, 1).astype(jnp.bfloat16)
    kept, given = partial_acts[:, :tokens], partial_acts[:, tokens:]
    partial_acts = in_order(kept, swap(given, "co"), core, 0)
    partial_acts = partial_acts.reshape(2, 4, 2, 2, features, tokens)
    partial_acts = partial_acts.transpose(1, 0, 3, 2, 4, 5).reshape(16, 2, features, tokens)
    shares = lax.all_to_all(partial_acts, ("y", "x"), 0, 0)
    shares = jnp.sum(shares.astype(jnp.float32), 0)
    away = swap(shares[1 - half].astype(jnp.bfloat16), "zh")
    grad_acts = (shares[half] + away.astype(jnp.float32)).astype(jnp.bfloat16).T

    grads = line_scatter(parts, place, {3: (shares,), 5: (away,)}).astype(jnp.bfloat16)
    return (
        grad_acts,
        grads[:, :units],
        grads[:, units : 2 * units],
        grads[:, 2 * units :].T,
    )


def solution(mesh):
    fine = Mesh(mesh.devices.reshape(ZL, 2, 4, 2, 4), ("zl", "co", "y", "zh", "x"))
    dp, mp = ("zl", "co"), ("y", "zh", "x")
    return jax.shard_map(
        per_device,
        mesh=fine,
        in_specs=(P(dp, mp), P(None, dp, mp), P(dp, mp), P(dp, mp), P(mp, dp), P(mp)),
        out_specs=(P(dp, mp), P(dp, mp), P(dp, mp), P(mp, dp)),
        check_vma=False,
    )
```

```python
import jax
import jax.numpy as jnp
from jax import lax
from jax.sharding import Mesh, PartitionSpec as P

FF = 10752
ZL = 8
GELU_SCALE = 0.7978845608028654


def gelu_parts(values):
    tanh_arg = GELU_SCALE * (values + 0.044715 * values * values * values)
    tanh_val = jnp.tanh(tanh_arg)
    activated = 0.5 * values * (1.0 + tanh_val)
    slope = 0.5 * (1.0 + tanh_val) + 0.5 * values * (1.0 - tanh_val * tanh_val) * GELU_SCALE * (
        1.0 + 3.0 * 0.044715 * values * values
    )
    return activated, slope


def dot(left, right, left_dim, right_dim):
    return lax.dot_general(
        left, right, (((left_dim,), (right_dim,)), ((), ())), preferred_element_type=jnp.float32
    )


def suffix_sums(cot_all):
    third = cot_all[3].astype(jnp.float32)
    second = cot_all[2].astype(jnp.float32) + third
    first = cot_all[1].astype(jnp.float32) + second
    zeroth = cot_all[0].astype(jnp.float32) + first
    return [part.astype(jnp.bfloat16) for part in (zeroth, first, second, third)]


def in_order(mine, other, index, axis):
    first = jnp.where(index == 0, mine, other)
    second = jnp.where(index == 0, other, mine)
    return jnp.stack([first, second], axis)


def swap(values, axis_name):
    return lax.ppermute(values, axis_name, [(0, 1), (1, 0)])


def step_round(values, axis_name, by):
    return lax.ppermute(values, axis_name, [(i, (i + by) % 4) for i in range(4)])


def around(blocks, place):
    twice = jnp.concatenate([blocks, blocks[:3]], 0)
    return lax.dynamic_slice_in_dim(twice, (4 - place) % 4, 4, 0)


class Beside:
    def __init__(self, stages):
        self.stages = stages
        self.result = None
        self.waiting = next(stages)

    def resume(self, arrays):
        if self.result is not None:
            return
        try:
            self.waiting = self.stages.send(arrays)
        except StopIteration as stop:
            self.waiting, self.result = (), stop.value

    def finish(self):
        while self.result is None:
            self.resume(self.waiting)
        return self.result


def gather_inputs(local, core):
    y, x = lax.axis_index("y"), lax.axis_index("x")

    def halves(blocks):
        kept = lax.dynamic_slice_in_dim(blocks, 2 * core, 2, 1)
        return kept, swap(lax.dynamic_slice_in_dim(blocks, 2 - 2 * core, 2, 1), "co")

    far = swap(local, "zh")
    right, left = step_round(local, "x", 1), step_round(local, "x", -1)
    right, left = yield right, left
    over = step_round(right, "x", 1)
    over, far = yield over, far
    near = around(jnp.stack([local, left, over, right]), x)
    up, down = step_round(near, "y", 1), step_round(near, "y", -1)
    right = step_round(far, "x", 1)
    up, down, right = yield up, down, right
    over_y = step_round(up, "y", 1)
    left, over = step_round(far, "x", -1), step_round(right, "x", 1)
    over_y, left, over = yield over_y, left, over
    far = around(jnp.stack([far, left, over, right]), x)
    kept, got = halves(jnp.stack([near, down, over_y, up]))
    up, down = step_round(far, "y", 1), step_round(far, "y", -1)
    up, down, got = yield up, down, got
    over_y = step_round(up, "y", 1)
    near = around(jnp.concatenate([kept, got], -1), y)
    over_y, near = yield over_y, near
    kept, got = halves(jnp.stack([far, down, over_y, up]))
    (got,) = yield (got,)
    return near, around(jnp.concatenate([kept, got], -1), y)


def scatter_acts(partial, core):
    tokens = partial.shape[1] // 2
    half = lax.axis_index("zh")
    kept, got = partial[:, :tokens], swap(partial[:, tokens:], "co")
    (got,) = yield (got,)
    blocks = in_order(kept, got, core, 0).reshape(2, 4, 2, 2, -1, tokens)
    blocks = blocks.transpose(1, 0, 3, 2, 4, 5).reshape(4, 4, 2, -1, tokens)
    for axis_name in ("y", "x"):
        place = lax.axis_index(axis_name)
        left = step_round(blocks[(place + 3) % 4].astype(jnp.bfloat16), axis_name, -1)
        (left,) = yield (left,)
        over = step_round(blocks[(place + 2) % 4].astype(jnp.bfloat16), axis_name, 1)
        (over,) = yield (over,)
        right = blocks[(place + 1) % 4].astype(jnp.float32) + over.astype(jnp.float32)
        right = step_round(right.astype(jnp.bfloat16), axis_name, 1)
        (right,) = yield (right,)
        blocks = blocks[place].astype(jnp.float32) + left.astype(jnp.float32)
        blocks = blocks + right.astype(jnp.float32)
    away = swap(blocks[1 - half].astype(jnp.bfloat16), "zh")
    (away,) = yield (away,)
    return (blocks[half] + away.astype(jnp.float32)).astype(jnp.bfloat16).T


def line_gather(shard, place, beside):
    from_left, from_right = [], []
    right = left = shard
    for step in range(ZL - 1):
        if step:
            right, left, tied = lax.optimization_barrier((right, left, beside.waiting))
            beside.resume(tied)
        right = lax.ppermute(right, "zl", [(i, i + 1) for i in range(step, ZL - 1)])
        left = lax.ppermute(left, "zl", [(i, i - 1) for i in range(1, ZL - step)])
        from_left.append(right)
        from_right.append(left)
    slots = jnp.stack(from_left[::-1] + [shard] + from_right)
    return lax.dynamic_slice_in_dim(slots, ZL - 1 - place, ZL, 0)


def line_scatter(parts, place, beside):
    rows = parts.shape[1]
    cut = rows // 16 * 8
    sent = []
    for turn in range(2 * (ZL - 1)):
        step = turn // 2
        low, high = ((0, cut), (cut, rows))[turn % 2]
        to_right = parts[jnp.clip(place + ZL - 1 - step, 0, ZL - 1), low:high]
        to_left = parts[jnp.clip(place - ZL + 1 + step, 0, ZL - 1), low:high]
        if step:
            to_right = to_right.astype(jnp.float32) + sent[turn - 2][0].astype(jnp.float32)
            to_left = to_left.astype(jnp.float32) + sent[turn - 2][1].astype(jnp.float32)
        to_right, to_left = to_right.astype(jnp.bfloat16), to_left.astype(jnp.bfloat16)
        before = sent[turn - 3] if turn > 2 else ()
        if turn:
            to_right, to_left, before, tied = lax.optimization_barrier(
                (to_right, to_left, before, beside.waiting)
            )
            beside.resume(tied)
        sent.append(
            (
                lax.ppermute(to_right, "zl", [(i, i + 1) for i in range(step + 1)]),
                lax.ppermute(to_left, "zl", [(i, i - 1) for i in range(ZL - 1 - step, ZL)]),
            )
        )
    total = parts[place].astype(jnp.float32)
    for way in range(2):
        total = total + jnp.concatenate([sent[-2][way], sent[-1][way]], 0).astype(jnp.float32)
    return total


def per_device(acts, cotangents, w_gate, w_up, w_down, unit_rank):
    place = lax.axis_index("zl")
    core = lax.axis_index("co")
    half = lax.axis_index("zh")
    tokens = acts.shape[0]
    units = unit_rank.shape[0]
    rows = w_gate.shape[0]

    local = jnp.concatenate([acts.T] + [part.T for part in suffix_sums(cotangents)], 1)
    beside = Beside(gather_inputs(local, core))
    weights = line_gather(jnp.concatenate([w_gate, w_up, w_down.T], 1), place, beside)
    weights = weights.reshape(ZL * rows, 3 * units)
    near, far = beside.finish()
    inputs = in_order(near, far, half, 1).reshape(ZL * rows, 10 * tokens)

    band = (
        (unit_rank >= FF // 8).astype(jnp.int32)
        + (unit_rank >= FF // 4).astype(jnp.int32)
        + (unit_rank >= FF // 2).astype(jnp.int32)
    )[None, :]
    products = dot(inputs, weights, 0, 0).reshape(2, 5, tokens, 3 * units)

    def of_bands(group):
        total = jnp.zeros((tokens, units), jnp.float32)
        for branch in range(4):
            total = jnp.where(band == branch, products[group, branch + 1, :, 2 * units :], total)
        return jnp.concatenate([products[group, 0, :, : 2 * units], total], 1)

    sums = of_bands(0) + swap(of_bands(1), "co")
    gate_proj, up_proj, grad_hidden = jnp.split(sums, 3, 1)
    activated, slope = gelu_parts(gate_proj)
    hidden = (activated * up_proj).astype(jnp.bfloat16)
    grad_gate_hidden = (grad_hidden * up_proj * slope).astype(jnp.bfloat16)
    grad_up_hidden = (grad_hidden * activated).astype(jnp.bfloat16)
    own = jnp.concatenate([grad_gate_hidden, grad_up_hidden, hidden], 1)
    other = swap(own, "co")

    def widened(values):
        up_to = jnp.pad(values[:, : 2 * units], ((0, 0), (0, units)))
        masked = [
            jnp.where(band == branch, values[:, 2 * units :], jnp.zeros((), values.dtype))
            for branch in range(4)
        ]
        return [up_to, jnp.pad(jnp.concatenate(masked, 0), ((0, 0), (2 * units, 0)))]

    wide = jnp.concatenate(widened(own) + widened(other), 0)
    parts = dot(inputs, wide, 1, 0).astype(jnp.bfloat16).reshape(ZL, rows, 3 * units)

    gate_up = jnp.concatenate([own[:, : 2 * units], other[:, : 2 * units]], 0)
    partial_acts = dot(weights[:, : 2 * units], gate_up, 1, 1).astype(jnp.bfloat16)
    beside = Beside(scatter_acts(partial_acts, core))
    grads = line_scatter(parts, place, beside).astype(jnp.bfloat16)
    grad_acts = beside.finish()
    return (
        grad_acts,
        grads[:, :units],
        grads[:, units : 2 * units],
        grads[:, 2 * units :].T,
    )


def solution(mesh):
    fine = Mesh(mesh.devices.reshape(ZL, 2, 4, 2, 4), ("zl", "co", "y", "zh", "x"))
    dp, mp = ("zl", "co"), ("y", "zh", "x")
    return jax.shard_map(
        per_device,
        mesh=fine,
        in_specs=(P(dp, mp), P(None, dp, mp), P(dp, mp), P(dp, mp), P(mp, dp), P(mp)),
        out_specs=(P(dp, mp), P(dp, mp), P(dp, mp), P(mp, dp)),
        check_vma=False,
    )
```

```python
import jax
import jax.numpy as jnp
from jax import lax
from jax.sharding import Mesh, PartitionSpec as P

FF = 10752
ZL = 8
GELU_SCALE = 0.7978845608028654


def gelu_parts(values):
    tanh_arg = GELU_SCALE * (values + 0.044715 * values * values * values)
    tanh_val = jnp.tanh(tanh_arg)
    activated = 0.5 * values * (1.0 + tanh_val)
    slope = 0.5 * (1.0 + tanh_val) + 0.5 * values * (1.0 - tanh_val * tanh_val) * GELU_SCALE * (
        1.0 + 3.0 * 0.044715 * values * values
    )
    return activated, slope


def dot(left, right, left_dim, right_dim):
    return lax.dot_general(
        left, right, (((left_dim,), (right_dim,)), ((), ())), preferred_element_type=jnp.float32
    )


def suffix_sums(cot_all):
    third = cot_all[3].astype(jnp.float32)
    second = cot_all[2].astype(jnp.float32) + third
    first = cot_all[1].astype(jnp.float32) + second
    zeroth = cot_all[0].astype(jnp.float32) + first
    return [part.astype(jnp.bfloat16) for part in (zeroth, first, second, third)]


def in_order(mine, other, index, axis):
    first = jnp.where(index == 0, mine, other)
    second = jnp.where(index == 0, other, mine)
    return jnp.stack([first, second], axis)


def swap(values, axis_name):
    return lax.ppermute(values, axis_name, [(0, 1), (1, 0)])


def line_step(values, by):
    return lax.ppermute(values, "zl", [(i, i + by) for i in range(ZL) if 0 <= i + by < ZL])


def step_round(values, axis_name, by):
    return lax.ppermute(values, axis_name, [(i, (i + by) % 4) for i in range(4)])


def around(blocks, place):
    twice = jnp.concatenate([blocks, blocks[:3]], 0)
    return lax.dynamic_slice_in_dim(twice, (4 - place) % 4, 4, 0)


class Beside:
    def __init__(self, stages):
        self.stages = stages
        self.result = None
        self.waiting = next(stages)

    def resume(self, arrays):
        if self.result is not None:
            return
        try:
            self.waiting = self.stages.send(arrays)
        except StopIteration as stop:
            self.waiting, self.result = (), stop.value

    def finish(self):
        while self.result is None:
            self.resume(self.waiting)
        return self.result


def gather_inputs(local, core):
    y, x = lax.axis_index("y"), lax.axis_index("x")

    def halves(blocks):
        kept = lax.dynamic_slice_in_dim(blocks, 2 * core, 2, 1)
        return kept, swap(lax.dynamic_slice_in_dim(blocks, 2 - 2 * core, 2, 1), "co")

    far = swap(local, "zh")
    right, left = step_round(local, "x", 1), step_round(local, "x", -1)
    right, left = yield right, left
    over = step_round(right, "x", 1)
    over, far = yield over, far
    near = around(jnp.stack([local, left, over, right]), x)
    up, down = step_round(near, "y", 1), step_round(near, "y", -1)
    right = step_round(far, "x", 1)
    up, down, right = yield up, down, right
    over_y = step_round(up, "y", 1)
    left, over = step_round(far, "x", -1), step_round(right, "x", 1)
    over_y, left, over = yield over_y, left, over
    far = around(jnp.stack([far, left, over, right]), x)
    kept, got = halves(jnp.stack([near, down, over_y, up]))
    up, down = step_round(far, "y", 1), step_round(far, "y", -1)
    up, down, got = yield up, down, got
    over_y = step_round(up, "y", 1)
    near = around(jnp.concatenate([kept, got], -1), y)
    over_y, near = yield over_y, near
    kept, got = halves(jnp.stack([far, down, over_y, up]))
    (got,) = yield (got,)
    return near, around(jnp.concatenate([kept, got], -1), y)


def scatter_acts(partial, core):
    tokens = partial.shape[1] // 2
    half = lax.axis_index("zh")
    kept, got = partial[:, :tokens], swap(partial[:, tokens:], "co")
    (got,) = yield (got,)
    blocks = in_order(kept, got, core, 0).reshape(2, 4, 2, 2, -1, tokens)
    blocks = blocks.transpose(1, 0, 3, 2, 4, 5).reshape(4, 4, 2, -1, tokens)
    for axis_name in ("y", "x"):
        place = lax.axis_index(axis_name)
        left = step_round(blocks[(place + 3) % 4].astype(jnp.bfloat16), axis_name, -1)
        (left,) = yield (left,)
        over = step_round(blocks[(place + 2) % 4].astype(jnp.bfloat16), axis_name, 1)
        (over,) = yield (over,)
        right = blocks[(place + 1) % 4].astype(jnp.float32) + over.astype(jnp.float32)
        right = step_round(right.astype(jnp.bfloat16), axis_name, 1)
        (right,) = yield (right,)
        blocks = blocks[place].astype(jnp.float32) + left.astype(jnp.float32)
        blocks = blocks + right.astype(jnp.float32)
    away = swap(blocks[1 - half].astype(jnp.bfloat16), "zh")
    (away,) = yield (away,)
    return (blocks[half] + away.astype(jnp.float32)).astype(jnp.bfloat16).T


def line_gather(shard, place, beside):
    from_left, from_right = [], []
    right = left = shard
    for step in range(ZL - 1):
        if step:
            right, left, tied = lax.optimization_barrier((right, left, beside.waiting))
            beside.resume(tied)
        right = line_step(right, 1)
        left = line_step(left, -1)
        from_left.append(right)
        from_right.append(left)
    slots = jnp.stack(from_left[::-1] + [shard] + from_right)
    return lax.dynamic_slice_in_dim(slots, ZL - 1 - place, ZL, 0)


def line_scatter(parts, place, beside):
    rows = parts.shape[1]
    cut = rows // 16 * 8
    sent = []
    for turn in range(2 * (ZL - 1)):
        step = turn // 2
        low, high = ((0, cut), (cut, rows))[turn % 2]
        to_right = parts[jnp.clip(place + ZL - 1 - step, 0, ZL - 1), low:high]
        to_left = parts[jnp.clip(place - ZL + 1 + step, 0, ZL - 1), low:high]
        if step:
            to_right = to_right.astype(jnp.float32) + sent[turn - 2][0].astype(jnp.float32)
            to_left = to_left.astype(jnp.float32) + sent[turn - 2][1].astype(jnp.float32)
        to_right, to_left = to_right.astype(jnp.bfloat16), to_left.astype(jnp.bfloat16)
        before = sent[turn - 3] if turn > 2 else ()
        if turn:
            to_right, to_left, before, tied = lax.optimization_barrier(
                (to_right, to_left, before, beside.waiting)
            )
            beside.resume(tied)
        sent.append(
            (
                line_step(to_right, 1),
                line_step(to_left, -1),
            )
        )
    total = parts[place].astype(jnp.float32)
    for way in range(2):
        total = total + jnp.concatenate([sent[-2][way], sent[-1][way]], 0).astype(jnp.float32)
    return total


def per_device(acts, cotangents, w_gate, w_up, w_down, unit_rank):
    place = lax.axis_index("zl")
    core = lax.axis_index("co")
    half = lax.axis_index("zh")
    tokens = acts.shape[0]
    units = unit_rank.shape[0]
    rows = w_gate.shape[0]

    local = jnp.concatenate([acts.T] + [part.T for part in suffix_sums(cotangents)], 1)
    beside = Beside(gather_inputs(local, core))
    weights = line_gather(jnp.concatenate([w_gate, w_up, w_down.T], 1), place, beside)
    weights = weights.reshape(ZL * rows, 3 * units)
    near, far = beside.finish()
    inputs = in_order(near, far, half, 1).reshape(ZL * rows, 10 * tokens)

    band = (
        (unit_rank >= FF // 8).astype(jnp.int32)
        + (unit_rank >= FF // 4).astype(jnp.int32)
        + (unit_rank >= FF // 2).astype(jnp.int32)
    )[None, :]
    products = dot(inputs, weights, 0, 0).reshape(2, 5, tokens, 3 * units)

    def of_bands(group):
        total = jnp.zeros((tokens, units), jnp.float32)
        for branch in range(4):
            total = jnp.where(band == branch, products[group, branch + 1, :, 2 * units :], total)
        return jnp.concatenate([products[group, 0, :, : 2 * units], total], 1)

    sums = of_bands(0) + swap(of_bands(1), "co")
    gate_proj, up_proj, grad_hidden = jnp.split(sums, 3, 1)
    activated, slope = gelu_parts(gate_proj)
    hidden = (activated * up_proj).astype(jnp.bfloat16)
    grad_gate_hidden = (grad_hidden * up_proj * slope).astype(jnp.bfloat16)
    grad_up_hidden = (grad_hidden * activated).astype(jnp.bfloat16)
    own = jnp.concatenate([grad_gate_hidden, grad_up_hidden, hidden], 1)
    other = swap(own, "co")

    def widened(values):
        up_to = jnp.pad(values[:, : 2 * units], ((0, 0), (0, units)))
        masked = [
            jnp.where(band == branch, values[:, 2 * units :], jnp.zeros((), values.dtype))
            for branch in range(4)
        ]
        return [up_to, jnp.pad(jnp.concatenate(masked, 0), ((0, 0), (2 * units, 0)))]

    wide = jnp.concatenate(widened(own) + widened(other), 0)
    parts = dot(inputs, wide, 1, 0).astype(jnp.bfloat16).reshape(ZL, rows, 3 * units)

    gate_up = jnp.concatenate([own[:, : 2 * units], other[:, : 2 * units]], 0)
    partial_acts = dot(weights[:, : 2 * units], gate_up, 1, 1).astype(jnp.bfloat16)
    beside = Beside(scatter_acts(partial_acts, core))
    grads = line_scatter(parts, place, beside).astype(jnp.bfloat16)
    grad_acts = beside.finish()
    return (
        grad_acts,
        grads[:, :units],
        grads[:, units : 2 * units],
        grads[:, 2 * units :].T,
    )


def solution(mesh):
    fine = Mesh(mesh.devices.reshape(ZL, 2, 4, 2, 4), ("zl", "co", "y", "zh", "x"))
    dp, mp = ("zl", "co"), ("y", "zh", "x")
    return jax.shard_map(
        per_device,
        mesh=fine,
        in_specs=(P(dp, mp), P(None, dp, mp), P(dp, mp), P(dp, mp), P(mp, dp), P(mp)),
        out_specs=(P(dp, mp), P(dp, mp), P(dp, mp), P(mp, dp)),
        check_vma=False,
    )
```

```python
import jax
import jax.numpy as jnp
from jax import lax
from jax.sharding import Mesh, PartitionSpec as P

FF = 10752
ZL = 8
GELU_SCALE = 0.7978845608028654


def gelu_parts(values):
    tanh_arg = GELU_SCALE * (values + 0.044715 * values * values * values)
    tanh_val = jnp.tanh(tanh_arg)
    activated = 0.5 * values * (1.0 + tanh_val)
    slope = 0.5 * (1.0 + tanh_val) + 0.5 * values * (1.0 - tanh_val * tanh_val) * GELU_SCALE * (
        1.0 + 3.0 * 0.044715 * values * values
    )
    return activated, slope


def dot(left, right, left_dim, right_dim):
    return lax.dot_general(
        left, right, (((left_dim,), (right_dim,)), ((), ())), preferred_element_type=jnp.float32
    )


def suffix_sums(cot_all):
    third = cot_all[3].astype(jnp.float32)
    second = cot_all[2].astype(jnp.float32) + third
    first = cot_all[1].astype(jnp.float32) + second
    zeroth = cot_all[0].astype(jnp.float32) + first
    return [part.astype(jnp.bfloat16) for part in (zeroth, first, second, third)]


def in_order(mine, other, index, axis):
    first = jnp.where(index == 0, mine, other)
    second = jnp.where(index == 0, other, mine)
    return jnp.stack([first, second], axis)


def swap(values, axis_name):
    return lax.ppermute(values, axis_name, [(0, 1), (1, 0)])


def line_gather(shard, place, stages):
    from_left, from_right = [], []
    right = left = shard
    waiting = next(stages)
    for step in range(ZL - 1):
        right, left, waiting = lax.optimization_barrier((right, left, waiting))
        if step < ZL - 2:
            waiting = stages.send(waiting)
        right = lax.ppermute(right, "zl", [(i, i + 1) for i in range(step, ZL - 1)])
        left = lax.ppermute(left, "zl", [(i, i - 1) for i in range(1, ZL - step)])
        from_left.append(right)
        from_right.append(left)
    slots = jnp.stack(from_left[::-1] + [shard] + from_right)
    return lax.dynamic_slice_in_dim(slots, ZL - 1 - place, ZL, 0), waiting


def line_scatter(parts, place, ties):
    right = left = None
    for step in range(ZL - 1):
        to_right = parts[jnp.clip(place + ZL - 1 - step, 0, ZL - 1)]
        to_left = parts[jnp.clip(place - ZL + 1 + step, 0, ZL - 1)]
        if step:
            to_right = to_right.astype(jnp.float32) + right.astype(jnp.float32)
            to_left = to_left.astype(jnp.float32) + left.astype(jnp.float32)
        to_right, to_left = to_right.astype(jnp.bfloat16), to_left.astype(jnp.bfloat16)
        if step in (4, ZL - 2):
            to_right, to_left, ties = lax.optimization_barrier((to_right, to_left, ties))
        else:
            to_right, to_left = lax.optimization_barrier((to_right, to_left))
        right = lax.ppermute(to_right, "zl", [(i, i + 1) for i in range(step + 1)])
        left = lax.ppermute(to_left, "zl", [(i, i - 1) for i in range(ZL - 1 - step, ZL)])
    total = parts[place].astype(jnp.float32)
    return total + right.astype(jnp.float32) + left.astype(jnp.float32), ties


def per_device(acts, cotangents, w_gate, w_up, w_down, unit_rank):
    place = lax.axis_index("zl")
    core = lax.axis_index("co")
    half = lax.axis_index("zh")
    tokens, features = acts.shape
    units = unit_rank.shape[0]
    rows = w_gate.shape[0]

    local = jnp.concatenate([acts.T] + [part.T for part in suffix_sums(cotangents)], 1)
    def spread(values):
        copies = jnp.broadcast_to(values[None], (16,) + values.shape)
        got = lax.all_to_all(copies, ("y", "x"), 0, 0)
        return got.reshape((4, 2, 2) + values.shape)

    def both_tokens(values):
        kept = lax.dynamic_index_in_dim(values, core, 1, False)
        given = lax.dynamic_index_in_dim(values, 1 - core, 1, False)
        return kept, swap(given, "co")

    def gathers():
        far = swap(local, "zh")
        near = spread(local)
        (far,) = yield (far,)
        far, near = yield far, near
        far = spread(far)
        near = both_tokens(near)
        (near,) = yield (near,)
        (near,) = yield (near,)
        far, near = yield far, near
        far, near = yield both_tokens(far), near
        parts = in_order(jnp.concatenate(near, -1), jnp.concatenate(far, -1), half, 1)
        yield parts.reshape(ZL * rows, 10 * tokens)

    weights, inputs = line_gather(
        jnp.concatenate([w_gate, w_up, w_down.T], 1), place, gathers()
    )
    weights = weights.reshape(ZL * rows, 3 * units)

    band = (
        (unit_rank >= FF // 8).astype(jnp.int32)
        + (unit_rank >= FF // 4).astype(jnp.int32)
        + (unit_rank >= FF // 2).astype(jnp.int32)
    )[None, :]
    products = dot(inputs, weights, 0, 0).reshape(2, 5, tokens, 3 * units)

    def of_bands(group):
        total = jnp.zeros((tokens, units), jnp.float32)
        for branch in range(4):
            total = jnp.where(band == branch, products[group, branch + 1, :, 2 * units :], total)
        return jnp.concatenate([products[group, 0, :, : 2 * units], total], 1)

    sums = of_bands(0) + swap(of_bands(1), "co")
    gate_proj, up_proj, grad_hidden = jnp.split(sums, 3, 1)
    activated, slope = gelu_parts(gate_proj)
    hidden = (activated * up_proj).astype(jnp.bfloat16)
    grad_gate_hidden = (grad_hidden * up_proj * slope).astype(jnp.bfloat16)
    grad_up_hidden = (grad_hidden * activated).astype(jnp.bfloat16)
    own = jnp.concatenate([grad_gate_hidden, grad_up_hidden, hidden], 1)
    other = swap(own, "co")

    def widened(values):
        up_to = jnp.pad(values[:, : 2 * units], ((0, 0), (0, units)))
        masked = [
            jnp.where(band == branch, values[:, 2 * units :], jnp.zeros((), values.dtype))
            for branch in range(4)
        ]
        return [up_to, jnp.pad(jnp.concatenate(masked, 0), ((0, 0), (2 * units, 0)))]

    wide = jnp.concatenate(widened(own) + widened(other), 0)
    parts = dot(inputs, wide, 1, 0).astype(jnp.bfloat16).reshape(ZL, rows, 3 * units)

    gate_up = jnp.concatenate([own[:, : 2 * units], other[:, : 2 * units]], 0)
    partial_acts = dot(weights[:, : 2 * units], gate_up, 1, 1).astype(jnp.bfloat16)
    kept, given = partial_acts[:, :tokens], partial_acts[:, tokens:]
    partial_acts = in_order(kept, swap(given, "co"), core, 0)
    partial_acts = partial_acts.reshape(2, 4, 2, 2, features, tokens)
    partial_acts = partial_acts.transpose(1, 0, 3, 2, 4, 5).reshape(16, 2, features, tokens)
    shares = lax.all_to_all(partial_acts, ("y", "x"), 0, 0)
    shares = jnp.sum(shares.astype(jnp.float32), 0)
    grads, (shares,) = line_scatter(parts, place, (shares,))
    grads = grads.astype(jnp.bfloat16)
    away = swap(shares[1 - half].astype(jnp.bfloat16), "zh")
    grad_acts = (shares[half] + away.astype(jnp.float32)).astype(jnp.bfloat16).T
    return (
        grad_acts,
        grads[:, :units],
        grads[:, units : 2 * units],
        grads[:, 2 * units :].T,
    )


def solution(mesh):
    fine = Mesh(mesh.devices.reshape(ZL, 2, 4, 2, 4), ("zl", "co", "y", "zh", "x"))
    dp, mp = ("zl", "co"), ("y", "zh", "x")
    return jax.shard_map(
        per_device,
        mesh=fine,
        in_specs=(P(dp, mp), P(None, dp, mp), P(dp, mp), P(dp, mp), P(mp, dp), P(mp)),
        out_specs=(P(dp, mp), P(dp, mp), P(dp, mp), P(mp, dp)),
        check_vma=False,
    )
```

```python
import jax
import jax.numpy as jnp
from jax import lax
from jax.sharding import Mesh, PartitionSpec as P

FF = 10752
ZL = 8
GELU_SCALE = 0.7978845608028654


def gelu_parts(values):
    tanh_arg = GELU_SCALE * (values + 0.044715 * values * values * values)
    tanh_val = jnp.tanh(tanh_arg)
    activated = 0.5 * values * (1.0 + tanh_val)
    slope = 0.5 * (1.0 + tanh_val) + 0.5 * values * (1.0 - tanh_val * tanh_val) * GELU_SCALE * (
        1.0 + 3.0 * 0.044715 * values * values
    )
    return activated, slope


def dot(left, right, left_dim, right_dim):
    return lax.dot_general(
        left, right, (((left_dim,), (right_dim,)), ((), ())), preferred_element_type=jnp.float32
    )


def suffix_sums(cot_all):
    third = cot_all[3].astype(jnp.float32)
    second = cot_all[2].astype(jnp.float32) + third
    first = cot_all[1].astype(jnp.float32) + second
    zeroth = cot_all[0].astype(jnp.float32) + first
    return [part.astype(jnp.bfloat16) for part in (zeroth, first, second, third)]


def in_order(mine, other, index, axis):
    first = jnp.where(index == 0, mine, other)
    second = jnp.where(index == 0, other, mine)
    return jnp.stack([first, second], axis)


def swap(values, axis_name):
    return lax.ppermute(values, axis_name, [(0, 1), (1, 0)])


def line_gather(shard, place, ties):
    from_left, from_right = [], []
    right = left = shard
    for step in range(ZL - 1):
        right, left, _ = lax.optimization_barrier((right, left, ties.get(step, ())))
        right = lax.ppermute(right, "zl", [(i, i + 1) for i in range(step, ZL - 1)])
        left = lax.ppermute(left, "zl", [(i, i - 1) for i in range(1, ZL - step)])
        from_left.append(right)
        from_right.append(left)
    slots = jnp.stack(from_left[::-1] + [shard] + from_right)
    return lax.dynamic_slice_in_dim(slots, ZL - 1 - place, ZL, 0)


def line_scatter(parts, place, ties):
    right = left = None
    for step in range(ZL - 1):
        to_right = parts[jnp.clip(place + ZL - 1 - step, 0, ZL - 1)]
        if step:
            to_right = to_right.astype(jnp.float32) + right.astype(jnp.float32)
        to_right, left, _ = lax.optimization_barrier(
            (to_right.astype(jnp.bfloat16), left, ties.get(step, ()))
        )
        right = lax.ppermute(to_right, "zl", [(i, i + 1) for i in range(step + 1)])
        to_left = parts[jnp.clip(place - ZL + 1 + step, 0, ZL - 1)]
        if step:
            to_left = to_left.astype(jnp.float32) + left.astype(jnp.float32)
        left = lax.ppermute(
            to_left.astype(jnp.bfloat16), "zl", [(i, i - 1) for i in range(ZL - 1 - step, ZL)]
        )
    return (
        parts[place].astype(jnp.float32) + right.astype(jnp.float32) + left.astype(jnp.float32)
    )


def per_device(acts, cotangents, w_gate, w_up, w_down, unit_rank):
    place = lax.axis_index("zl")
    core = lax.axis_index("co")
    half = lax.axis_index("zh")
    tokens, features = acts.shape
    units = unit_rank.shape[0]
    rows = w_gate.shape[0]

    local = jnp.concatenate([acts.T] + [part.T for part in suffix_sums(cotangents)], 1)
    far_local = swap(local, "zh")

    def spread(values):
        copies = jnp.broadcast_to(values[None], (16,) + values.shape)
        got = lax.all_to_all(copies, ("y", "x"), 0, 0)
        return got.reshape((4, 2, 2) + values.shape)

    def both_tokens(values):
        kept = lax.dynamic_index_in_dim(values, core, 1, False)
        given = lax.dynamic_index_in_dim(values, 1 - core, 1, False)
        return kept, swap(given, "co")

    near = spread(local)
    near_parts = both_tokens(near)
    far = spread(far_local)
    far_parts = both_tokens(far)
    inputs = in_order(
        jnp.concatenate(near_parts, -1), jnp.concatenate(far_parts, -1), half, 1
    ).reshape(ZL * rows, 10 * tokens)
    ties = {1: (far_local,), 3: (near,), 4: near_parts + (far,), 5: far_parts, 6: (inputs,)}

    weights = line_gather(jnp.concatenate([w_gate, w_up, w_down.T], 1), place, ties)
    weights = weights.reshape(ZL * rows, 3 * units)
    band = (
        (unit_rank >= FF // 8).astype(jnp.int32)
        + (unit_rank >= FF // 4).astype(jnp.int32)
        + (unit_rank >= FF // 2).astype(jnp.int32)
    )[None, :]
    products = dot(inputs, weights, 0, 0).reshape(2, 5, tokens, 3 * units)

    def of_bands(group):
        total = jnp.zeros((tokens, units), jnp.float32)
        for branch in range(4):
            total = jnp.where(band == branch, products[group, branch + 1, :, 2 * units :], total)
        return jnp.concatenate([products[group, 0, :, : 2 * units], total], 1)

    sums = of_bands(0) + swap(of_bands(1), "co")
    gate_proj, up_proj, grad_hidden = jnp.split(sums, 3, 1)
    activated, slope = gelu_parts(gate_proj)
    hidden = (activated * up_proj).astype(jnp.bfloat16)
    grad_gate_hidden = (grad_hidden * up_proj * slope).astype(jnp.bfloat16)
    grad_up_hidden = (grad_hidden * activated).astype(jnp.bfloat16)
    own = jnp.concatenate([grad_gate_hidden, grad_up_hidden, hidden], 1)
    other = swap(own, "co")

    def widened(values):
        up_to = jnp.pad(values[:, : 2 * units], ((0, 0), (0, units)))
        masked = [
            jnp.where(band == branch, values[:, 2 * units :], jnp.zeros((), values.dtype))
            for branch in range(4)
        ]
        return [up_to, jnp.pad(jnp.concatenate(masked, 0), ((0, 0), (2 * units, 0)))]

    wide = jnp.concatenate(widened(own) + widened(other), 0)
    parts = dot(inputs, wide, 1, 0).astype(jnp.bfloat16).reshape(ZL, rows, 3 * units)

    gate_up = jnp.concatenate([own[:, : 2 * units], other[:, : 2 * units]], 0)
    partial_acts = dot(weights[:, : 2 * units], gate_up, 1, 1).astype(jnp.bfloat16)
    kept, given = partial_acts[:, :tokens], partial_acts[:, tokens:]
    partial_acts = in_order(kept, swap(given, "co"), core, 0)
    partial_acts = partial_acts.reshape(2, 4, 2, 2, features, tokens)
    partial_acts = partial_acts.transpose(1, 0, 3, 2, 4, 5).reshape(16, 2, features, tokens)
    shares = lax.all_to_all(partial_acts, ("y", "x"), 0, 0)
    shares = jnp.sum(shares.astype(jnp.float32), 0)
    away = swap(shares[1 - half].astype(jnp.bfloat16), "zh")
    grad_acts = (shares[half] + away.astype(jnp.float32)).astype(jnp.bfloat16).T

    grads = line_scatter(parts, place, {3: (shares,), 5: (away,)}).astype(jnp.bfloat16)
    return (
        grad_acts,
        grads[:, :units],
        grads[:, units : 2 * units],
        grads[:, 2 * units :].T,
    )


def solution(mesh):
    fine = Mesh(mesh.devices.reshape(ZL, 2, 4, 2, 4), ("zl", "co", "y", "zh", "x"))
    dp, mp = ("zl", "co"), ("y", "zh", "x")
    return jax.shard_map(
        per_device,
        mesh=fine,
        in_specs=(P(dp, mp), P(None, dp, mp), P(dp, mp), P(dp, mp), P(mp, dp), P(mp)),
        out_specs=(P(dp, mp), P(dp, mp), P(dp, mp), P(mp, dp)),
        check_vma=False,
    )
```

```python
import jax
import jax.numpy as jnp
from jax import lax
from jax.sharding import Mesh, PartitionSpec as P

FF = 10752
ZL = 8
GELU_SCALE = 0.7978845608028654


def gelu_parts(values):
    tanh_arg = GELU_SCALE * (values + 0.044715 * values * values * values)
    tanh_val = jnp.tanh(tanh_arg)
    activated = 0.5 * values * (1.0 + tanh_val)
    slope = 0.5 * (1.0 + tanh_val) + 0.5 * values * (1.0 - tanh_val * tanh_val) * GELU_SCALE * (
        1.0 + 3.0 * 0.044715 * values * values
    )
    return activated, slope


def dot(left, right, left_dim, right_dim):
    return lax.dot_general(
        left, right, (((left_dim,), (right_dim,)), ((), ())), preferred_element_type=jnp.float32
    )


def suffix_sums(cot_all):
    third = cot_all[3].astype(jnp.float32)
    second = cot_all[2].astype(jnp.float32) + third
    first = cot_all[1].astype(jnp.float32) + second
    zeroth = cot_all[0].astype(jnp.float32) + first
    return [part.astype(jnp.bfloat16) for part in (zeroth, first, second, third)]


def in_order(mine, other, index, axis):
    first = jnp.where(index == 0, mine, other)
    second = jnp.where(index == 0, other, mine)
    return jnp.stack([first, second], axis)


def swap(values, axis_name):
    return lax.ppermute(values, axis_name, [(0, 1), (1, 0)])


def line_gather(shard, place, ties):
    from_left, from_right = [], []
    right = left = shard
    for step in range(ZL - 1):
        other = (from_left[step - 2], from_right[step - 2]) if step > 1 else ((), ())
        right, _ = lax.optimization_barrier((right, (other[1], ties.get(step, ()))))
        left, _ = lax.optimization_barrier((left, other[0]))
        right = lax.ppermute(right, "zl", [(i, i + 1) for i in range(step, ZL - 1)])
        left = lax.ppermute(left, "zl", [(i, i - 1) for i in range(1, ZL - step)])
        from_left.append(right)
        from_right.append(left)
    slots = jnp.stack(from_left[::-1] + [shard] + from_right)
    return lax.dynamic_slice_in_dim(slots, ZL - 1 - place, ZL, 0)


def line_scatter(parts, place, ties):
    right = left = None
    for step in range(ZL - 1):
        to_right = parts[jnp.clip(place + ZL - 1 - step, 0, ZL - 1)]
        to_left = parts[jnp.clip(place - ZL + 1 + step, 0, ZL - 1)]
        if step:
            to_right = to_right.astype(jnp.float32) + right.astype(jnp.float32)
            to_left = to_left.astype(jnp.float32) + left.astype(jnp.float32)
        to_right, to_left = to_right.astype(jnp.bfloat16), to_left.astype(jnp.bfloat16)
        to_right, to_left, _ = lax.optimization_barrier((to_right, to_left, ties.get(step, ())))
        right = lax.ppermute(to_right, "zl", [(i, i + 1) for i in range(step + 1)])
        left = lax.ppermute(to_left, "zl", [(i, i - 1) for i in range(ZL - 1 - step, ZL)])
    return (
        parts[place].astype(jnp.float32) + right.astype(jnp.float32) + left.astype(jnp.float32)
    )


def per_device(acts, cotangents, w_gate, w_up, w_down, unit_rank):
    place = lax.axis_index("zl")
    core = lax.axis_index("co")
    half = lax.axis_index("zh")
    tokens, features = acts.shape
    units = unit_rank.shape[0]
    rows = w_gate.shape[0]

    local = jnp.concatenate([acts.T] + [part.T for part in suffix_sums(cotangents)], 1)
    far_local = swap(local, "zh")

    def spread(values):
        copies = jnp.broadcast_to(values[None], (16,) + values.shape)
        got = lax.all_to_all(copies, ("y", "x"), 0, 0)
        return got.reshape((4, 2, 2) + values.shape)

    def both_tokens(values):
        kept = lax.dynamic_index_in_dim(values, core, 1, False)
        given = lax.dynamic_index_in_dim(values, 1 - core, 1, False)
        return kept, swap(given, "co")

    near = spread(local)
    near_parts = both_tokens(near)
    far = spread(far_local)
    far_parts = both_tokens(far)
    ties = {1: (far_local,), 3: (near,), 4: near_parts, 5: (far,), 6: far_parts}

    weights = line_gather(jnp.concatenate([w_gate, w_up, w_down.T], 1), place, ties)
    weights = weights.reshape(ZL * rows, 3 * units)
    inputs = in_order(
        jnp.concatenate(near_parts, -1), jnp.concatenate(far_parts, -1), half, 1
    ).reshape(ZL * rows, 10 * tokens)

    band = (
        (unit_rank >= FF // 8).astype(jnp.int32)
        + (unit_rank >= FF // 4).astype(jnp.int32)
        + (unit_rank >= FF // 2).astype(jnp.int32)
    )[None, :]
    products = dot(inputs, weights, 0, 0).reshape(2, 5, tokens, 3 * units)

    def of_bands(group):
        total = jnp.zeros((tokens, units), jnp.float32)
        for branch in range(4):
            total = jnp.where(band == branch, products[group, branch + 1, :, 2 * units :], total)
        return jnp.concatenate([products[group, 0, :, : 2 * units], total], 1)

    sums = of_bands(0) + swap(of_bands(1), "co")
    gate_proj, up_proj, grad_hidden = jnp.split(sums, 3, 1)
    activated, slope = gelu_parts(gate_proj)
    hidden = (activated * up_proj).astype(jnp.bfloat16)
    grad_gate_hidden = (grad_hidden * up_proj * slope).astype(jnp.bfloat16)
    grad_up_hidden = (grad_hidden * activated).astype(jnp.bfloat16)
    own = jnp.concatenate([grad_gate_hidden, grad_up_hidden, hidden], 1)
    other = swap(own, "co")

    def widened(values):
        up_to = jnp.pad(values[:, : 2 * units], ((0, 0), (0, units)))
        masked = [
            jnp.where(band == branch, values[:, 2 * units :], jnp.zeros((), values.dtype))
            for branch in range(4)
        ]
        return [up_to, jnp.pad(jnp.concatenate(masked, 0), ((0, 0), (2 * units, 0)))]

    wide = jnp.concatenate(widened(own) + widened(other), 0)
    parts = dot(inputs, wide, 1, 0).astype(jnp.bfloat16).reshape(ZL, rows, 3 * units)

    gate_up = jnp.concatenate([own[:, : 2 * units], other[:, : 2 * units]], 0)
    partial_acts = dot(weights[:, : 2 * units], gate_up, 1, 1).astype(jnp.bfloat16)
    kept, given = partial_acts[:, :tokens], partial_acts[:, tokens:]
    partial_acts = in_order(kept, swap(given, "co"), core, 0)
    partial_acts = partial_acts.reshape(2, 4, 2, 2, features, tokens)
    partial_acts = partial_acts.transpose(1, 0, 3, 2, 4, 5).reshape(16, 2, features, tokens)
    shares = lax.all_to_all(partial_acts, ("y", "x"), 0, 0)
    shares = jnp.sum(shares.astype(jnp.float32), 0)
    away = swap(shares[1 - half].astype(jnp.bfloat16), "zh")
    grad_acts = (shares[half] + away.astype(jnp.float32)).astype(jnp.bfloat16).T

    grads = line_scatter(parts, place, {3: (shares,), 5: (away,)}).astype(jnp.bfloat16)
    return (
        grad_acts,
        grads[:, :units],
        grads[:, units : 2 * units],
        grads[:, 2 * units :].T,
    )


def solution(mesh):
    fine = Mesh(mesh.devices.reshape(ZL, 2, 4, 2, 4), ("zl", "co", "y", "zh", "x"))
    dp, mp = ("zl", "co"), ("y", "zh", "x")
    return jax.shard_map(
        per_device,
        mesh=fine,
        in_specs=(P(dp, mp), P(None, dp, mp), P(dp, mp), P(dp, mp), P(mp, dp), P(mp)),
        out_specs=(P(dp, mp), P(dp, mp), P(dp, mp), P(mp, dp)),
        check_vma=False,
    )
```

```python
import jax
import jax.numpy as jnp
from jax import lax
from jax.sharding import Mesh, PartitionSpec as P

FF = 10752
ZL = 8
GELU_SCALE = 0.7978845608028654


def gelu_parts(values):
    tanh_arg = GELU_SCALE * (values + 0.044715 * values * values * values)
    tanh_val = jnp.tanh(tanh_arg)
    activated = 0.5 * values * (1.0 + tanh_val)
    slope = 0.5 * (1.0 + tanh_val) + 0.5 * values * (1.0 - tanh_val * tanh_val) * GELU_SCALE * (
        1.0 + 3.0 * 0.044715 * values * values
    )
    return activated, slope


def dot(left, right, left_dim, right_dim):
    return lax.dot_general(
        left, right, (((left_dim,), (right_dim,)), ((), ())), preferred_element_type=jnp.float32
    )


def suffix_sums(cot_all):
    third = cot_all[3].astype(jnp.float32)
    second = cot_all[2].astype(jnp.float32) + third
    first = cot_all[1].astype(jnp.float32) + second
    zeroth = cot_all[0].astype(jnp.float32) + first
    return [part.astype(jnp.bfloat16) for part in (zeroth, first, second, third)]


def in_order(mine, other, index, axis):
    first = jnp.where(index == 0, mine, other)
    second = jnp.where(index == 0, other, mine)
    return jnp.stack([first, second], axis)


def swap(values, axis_name):
    return lax.ppermute(values, axis_name, [(0, 1), (1, 0)])


def line_gather(shard, place, ties):
    from_left, from_right = [], []
    right = left = shard
    for step in range(ZL - 1):
        other = (from_left[step - 2], from_right[step - 2]) if step > 1 else ((), ())
        right, _ = lax.optimization_barrier((right, (other[1], ties.get(step, ()))))
        left, _ = lax.optimization_barrier((left, other[0]))
        right = lax.ppermute(right, "zl", [(i, i + 1) for i in range(step, ZL - 1)])
        left = lax.ppermute(left, "zl", [(i, i - 1) for i in range(1, ZL - step)])
        from_left.append(right)
        from_right.append(left)
    slots = jnp.stack(from_left[::-1] + [shard] + from_right)
    return lax.dynamic_slice_in_dim(slots, ZL - 1 - place, ZL, 0)


def line_scatter(parts, place, ties):
    right = left = None
    earlier = ((), ())
    for step in range(ZL - 1):
        to_right = parts[jnp.clip(place + ZL - 1 - step, 0, ZL - 1)]
        to_left = parts[jnp.clip(place - ZL + 1 + step, 0, ZL - 1)]
        if step:
            to_right = to_right.astype(jnp.float32) + right.astype(jnp.float32)
            to_left = to_left.astype(jnp.float32) + left.astype(jnp.float32)
        to_right, to_left = to_right.astype(jnp.bfloat16), to_left.astype(jnp.bfloat16)
        to_right, _ = lax.optimization_barrier((to_right, (earlier[1], ties.get(step, ()))))
        to_left, _ = lax.optimization_barrier((to_left, earlier[0]))
        earlier = (right, left) if step else ((), ())
        right = lax.ppermute(to_right, "zl", [(i, i + 1) for i in range(step + 1)])
        left = lax.ppermute(to_left, "zl", [(i, i - 1) for i in range(ZL - 1 - step, ZL)])
    return (
        parts[place].astype(jnp.float32) + right.astype(jnp.float32) + left.astype(jnp.float32)
    )


def per_device(acts, cotangents, w_gate, w_up, w_down, unit_rank):
    place = lax.axis_index("zl")
    core = lax.axis_index("co")
    half = lax.axis_index("zh")
    tokens, features = acts.shape
    units = unit_rank.shape[0]
    rows = w_gate.shape[0]

    local = jnp.concatenate([acts.T] + [part.T for part in suffix_sums(cotangents)], 1)
    far_local = swap(local, "zh")

    def spread(values):
        copies = jnp.broadcast_to(values[None], (16,) + values.shape)
        got = lax.all_to_all(copies, ("y", "x"), 0, 0)
        return got.reshape((4, 2, 2) + values.shape)

    def both_tokens(values):
        kept = lax.dynamic_index_in_dim(values, core, 1, False)
        given = lax.dynamic_index_in_dim(values, 1 - core, 1, False)
        return kept, swap(given, "co")

    near = spread(local)
    near_parts = both_tokens(near)
    far = spread(far_local)
    far_parts = both_tokens(far)
    ties = {1: (far_local,), 3: (near,), 4: near_parts, 5: (far,), 6: far_parts}

    weights = line_gather(jnp.concatenate([w_gate, w_up, w_down.T], 1), place, ties)
    weights = weights.reshape(ZL * rows, 3 * units)
    inputs = in_order(
        jnp.concatenate(near_parts, -1), jnp.concatenate(far_parts, -1), half, 1
    ).reshape(ZL * rows, 10 * tokens)

    band = (
        (unit_rank >= FF // 8).astype(jnp.int32)
        + (unit_rank >= FF // 4).astype(jnp.int32)
        + (unit_rank >= FF // 2).astype(jnp.int32)
    )[None, :]
    products = dot(inputs, weights, 0, 0).reshape(2, 5, tokens, 3 * units)

    def of_bands(group):
        total = jnp.zeros((tokens, units), jnp.float32)
        for branch in range(4):
            total = jnp.where(band == branch, products[group, branch + 1, :, 2 * units :], total)
        return jnp.concatenate([products[group, 0, :, : 2 * units], total], 1)

    sums = of_bands(0) + swap(of_bands(1), "co")
    gate_proj, up_proj, grad_hidden = jnp.split(sums, 3, 1)
    activated, slope = gelu_parts(gate_proj)
    hidden = (activated * up_proj).astype(jnp.bfloat16)
    grad_gate_hidden = (grad_hidden * up_proj * slope).astype(jnp.bfloat16)
    grad_up_hidden = (grad_hidden * activated).astype(jnp.bfloat16)
    own = jnp.concatenate([grad_gate_hidden, grad_up_hidden, hidden], 1)
    other = swap(own, "co")

    def widened(values):
        up_to = jnp.pad(values[:, : 2 * units], ((0, 0), (0, units)))
        masked = [
            jnp.where(band == branch, values[:, 2 * units :], jnp.zeros((), values.dtype))
            for branch in range(4)
        ]
        return [up_to, jnp.pad(jnp.concatenate(masked, 0), ((0, 0), (2 * units, 0)))]

    wide = jnp.concatenate(widened(own) + widened(other), 0)
    parts = dot(inputs, wide, 1, 0).astype(jnp.bfloat16).reshape(ZL, rows, 3 * units)

    gate_up = jnp.concatenate([own[:, : 2 * units], other[:, : 2 * units]], 0)
    partial_acts = dot(weights[:, : 2 * units], gate_up, 1, 1).astype(jnp.bfloat16)
    kept, given = partial_acts[:, :tokens], partial_acts[:, tokens:]
    partial_acts = in_order(kept, swap(given, "co"), core, 0)
    partial_acts = partial_acts.reshape(2, 4, 2, 2, features, tokens)
    partial_acts = partial_acts.transpose(1, 0, 3, 2, 4, 5).reshape(16, 2, features, tokens)
    shares = lax.all_to_all(partial_acts, ("y", "x"), 0, 0)
    shares = jnp.sum(shares.astype(jnp.float32), 0)
    away = swap(shares[1 - half].astype(jnp.bfloat16), "zh")
    grad_acts = (shares[half] + away.astype(jnp.float32)).astype(jnp.bfloat16).T

    grads = line_scatter(parts, place, {3: (shares,), 5: (away,)}).astype(jnp.bfloat16)
    return (
        grad_acts,
        grads[:, :units],
        grads[:, units : 2 * units],
        grads[:, 2 * units :].T,
    )


def solution(mesh):
    fine = Mesh(mesh.devices.reshape(ZL, 2, 4, 2, 4), ("zl", "co", "y", "zh", "x"))
    dp, mp = ("zl", "co"), ("y", "zh", "x")
    return jax.shard_map(
        per_device,
        mesh=fine,
        in_specs=(P(dp, mp), P(None, dp, mp), P(dp, mp), P(dp, mp), P(mp, dp), P(mp)),
        out_specs=(P(dp, mp), P(dp, mp), P(dp, mp), P(mp, dp)),
        check_vma=False,
    )
```
